32 devices in a mesh: groups: 2 (over y), seq: 16 (over z, x, core).
Axes of the slice: x: 2, y: 2, z: 4, core: 2. Of those that a mesh axis runs over, the one named last changes fastest.
Arguments:
- q_fresh: bfloat16 [2048, 5120], P(('groups', 'seq')), parts along dimension 0, may hold values from -48 to 48
- k_fresh: bfloat16 [2048, 5120], P(('groups', 'seq')), parts along dimension 0, may hold values from -48 to 48
- v_fresh: bfloat16 [2048, 5120], P(('groups', 'seq')), parts along dimension 0, may hold values from -6 to 6
- q_gain: bfloat16 [5120], replicated, may hold values from 1 to 4
- k_gain: bfloat16 [5120], replicated, may hold values from 0.5 to 2
- stale_keys: bfloat16 [32, 512, 640], P(('groups', 'seq')), parts along dimension 0, may hold values from -6 to 6
- stale_values: bfloat16 [32, 512, 640], P(('groups', 'seq')), parts along dimension 0, may hold values from -6 to 6
- gate_table: bfloat16 [50, 5120], replicated, may hold values from 0.5 to 3
- assign: int32 [32], P('groups'), parts along dimension 0, may hold values from 0 to 15, each once
- counts: int32 [32], P('groups'), parts along dimension 0, may hold values from 1 to 64, 768 in all
- timestep: int32 [2], P('groups'), parts along dimension 0, may hold values from 0 to 49
Outputs:
- mixed: bfloat16 [2048, 5120], P(('groups', 'seq')), parts along dimension 0
- new_keys: bfloat16 [32, 512, 640], P(('groups', 'seq')), parts along dimension 0
- new_values: bfloat16 [32, 512, 640], P(('groups', 'seq')), parts along dimension 0
The draws below stay inside these ranges and needn't reach their ends.
There are 2 independent parts, one for each index of `groups`. The reference program is written for one: setup_inputs(seed, part) draws one part's arguments, and reference() takes and returns one part's arrays. A program takes and returns all parts, laid end to end along the dimension named above; an argument that names none is the same for every part. Nothing has to cross between parts.
Inputs may be any that keep to these rules, and one draw needn't show every extreme that they name: Index i of seq holds the rows of patch assign[i]; every patch is held once. `counts`: some patch has all 64 tokens live.
All inputs are finite; a program needn't handle non-finite values.
Results may differ from the reference program's by a relative error of at most 0.011.
Values may be sent and summed in bfloat16 or wider, within the bound.
No kernel may reach another device: no remote copies, remote signals or barrier semaphores. Data moves between devices by JAX's collectives and lax.ppermute only.
A program may use at most 64 MiB of HBM per device.

```python
import math
import jax
import jax.numpy as jnp
import numpy as np
from jax import lax

D = 5120
HEADS = 40
HEAD = 128
GROUPS = 8
STEPS = 50
TOK_DEV = 64
HEADS_DEV = 5
BLOCK_TOK = 512
BLOCKS = 2
PATCHES = 16
SEQ = 1024
N_SEQ = 16


def draw_q_fresh(key, part):
    key = jax.random.fold_in(key, 7)
    drawn = jnp.clip(jax.random.normal(key, (SEQ, D), dtype=jnp.float32), -6.0, 6.0)
    return drawn.astype(jnp.bfloat16)


def draw_k_fresh(key, part):
    key = jax.random.fold_in(key, 8)
    drawn = jnp.clip(jax.random.normal(key, (SEQ, D), dtype=jnp.float32), -6.0, 6.0)
    return drawn.astype(jnp.bfloat16)


def levels(stream_key, extent, split, low, top_value):
    def one(axis_at, blocks):
        draws = jax.random.uniform(jax.random.fold_in(jax.random.fold_in(stream_key, 6), axis_at), (blocks,), jnp.float32, low / len(split), top_value / len(split))
        return jnp.repeat(jnp.exp(draws), extent[axis_at] // blocks).reshape((-1,) + (1,) * (len(extent) - axis_at - 1))

    gain = one(*split[0])
    for cut in split[1:]:
        gain = gain * one(*cut)
    return gain


def split_up(count, total, most, lean):
    portions = [(1 << 20) // math.isqrt(grade ** lean) + 1 for grade in range(2, count + 1)]
    spare, given = total - most - (count - 1), [1] * (count - 1)
    while spare > 0:
        candidates = [i for i in range(count - 1) if given[i] < most]
        whole, left = sum([portions[i] for i in candidates]), spare
        for i in candidates:
            more = min(most - given[i], max(1, left * portions[i] // whole), spare)
            given[i] = given[i] + more
            spare = spare - more
    return np.array([most] + given)


def ragged(stream_key, number_of, total, most, skew):
    if number_of == 2:
        one = jax.random.randint(stream_key, (), max(1, total - most), min(most, total - 1) + 1)
        return jnp.stack([one, total - one])
    tallies = jnp.asarray(split_up(number_of, total, most, skew), jnp.int32)
    couples = (number_of - 1) // 2
    giver, taker = tallies[1:1 + 2 * couples:2], tallies[2:2 + 2 * couples:2]
    room = jnp.minimum(giver - 1, most - taker)
    passed = jax.random.randint(jax.random.fold_in(stream_key, 1), (couples,), 0, 1 << 20) % (room + 1)
    tallies = tallies.at[1:1 + 2 * couples:2].set(giver - passed).at[2:2 + 2 * couples:2].set(taker + passed)
    return tallies[jax.random.permutation(jax.random.fold_in(stream_key, 2), number_of)]


def gaussian(stream_key, dims, width, most, shards=(), held_as=jnp.bfloat16):
    loudness = levels(stream_key, dims, shards, -0.22, 0.18) if shards else 1.0
    entries = jax.random.normal(stream_key, dims, jnp.float32) * width * loudness
    return jnp.minimum(jnp.maximum(entries, -most), most).astype(held_as)


def setup_inputs(seed: int = 0, part: int = 0) -> dict:
    splits = jax.random.split(jax.random.key(seed), 12)
    part_splits = jax.random.split(jax.random.fold_in(splits[11], part), 12)
    return {
        "q_fresh": draw_q_fresh(jax.random.fold_in(jax.random.fold_in(splits[11], part), 71), part),
        "k_fresh": draw_k_fresh(jax.random.fold_in(jax.random.fold_in(splits[11], part), 71), part),
        "v_fresh": gaussian(part_splits[2], (SEQ, D), 1.0, 6.0, ((0, 16),)),
        "q_gain": jnp.clip(jnp.exp(jax.random.uniform(splits[3], (D,), jnp.float32, math.log(1.0), math.log(4.0))), 1.0, 4.0).astype(jnp.bfloat16),
        "k_gain": jnp.clip(jnp.exp(jax.random.uniform(splits[4], (D,), jnp.float32, math.log(0.5), math.log(2.0))), 0.5, 2.0).astype(jnp.bfloat16),
        "stale_keys": gaussian(part_splits[5], (N_SEQ, BLOCK_TOK, HEADS_DEV * HEAD), 1.0, 6.0, ((0, 16),)),
        "stale_values": gaussian(part_splits[6], (N_SEQ, BLOCK_TOK, HEADS_DEV * HEAD), 1.0, 6.0, ((0, 16),)),
        "gate_table": jnp.clip(jax.random.uniform(splits[7], (STEPS, D), jnp.float32, 0.5, 3.0), 0.5, 3.0).astype(jnp.bfloat16),
        "assign": jax.random.permutation(part_splits[8], PATCHES).astype(jnp.int32),
        "counts": ragged(part_splits[9], PATCHES, PATCHES * TOK_DEV * 3 // 4, TOK_DEV, 1).astype(jnp.int32),
        "timestep": jax.random.randint(part_splits[10], (1,), 0, STEPS).astype(jnp.int32),
    }


rms_eps = 1e-06

def apply_rope(normed, positions):
    tok_rows = normed.shape[0]
    half_size = HEAD // 2
    paired = normed.reshape(tok_rows, -1, 2, half_size)
    angle_step = 10000.0 ** (-(jnp.arange(half_size, dtype=jnp.float32) * 2.0 / HEAD))
    angles = positions.astype(jnp.float32)[:, None] * angle_step[None, :]
    cos_part = jnp.cos(angles)[:, None, :]
    sin_part = jnp.sin(angles)[:, None, :]
    first_half = paired[:, :, 0]
    second_half = paired[:, :, 1]
    turned = jnp.stack([first_half * cos_part - second_half * sin_part, first_half * sin_part + second_half * cos_part], axis=2)
    return turned.reshape(tok_rows, -1)

def norm_rope(tokens, gain_vec, positions):
    as_float = tokens.astype(jnp.float32)
    mean_square = lax.optimization_barrier(jnp.mean(as_float * as_float, axis=-1, keepdims=True))
    normed = as_float * lax.rsqrt(mean_square + rms_eps) * gain_vec.astype(jnp.float32)
    return apply_rope(normed, positions).astype(jnp.bfloat16)

def reference(q_fresh, k_fresh, v_fresh, q_gain, k_gain, stale_keys, stale_values, gate_table, assign, counts, timestep):
    offsets = jnp.arange(TOK_DEV, dtype=jnp.int32)
    positions = (assign[:, None] * TOK_DEV + offsets[None, :]).reshape(SEQ).astype(jnp.int32)
    live_keys = (offsets[None, :] < counts[assign][:, None]).reshape(SEQ)
    query_rot = norm_rope(q_fresh, q_gain, positions)
    key_rot = norm_rope(k_fresh, k_gain, positions)

    def by_head(tokens):
        return tokens.reshape(BLOCKS, BLOCK_TOK, HEADS, HEAD).transpose(2, 0, 1, 3)

    def stale_by_head(cache):
        grid = cache.reshape(BLOCKS, GROUPS, BLOCK_TOK, HEADS_DEV, HEAD).transpose(1, 3, 0, 2, 4)
        return grid.reshape(HEADS, BLOCKS, BLOCK_TOK, HEAD)
    block_ids = jnp.arange(BLOCKS, dtype=jnp.int32)
    score_scale = HEAD ** (-0.5)

    def one_head(per_head):
        query_blocks, fresh_keys, fresh_values, old_keys, old_values = per_head

        def one_block(block_id):
            here_mask = (block_ids == block_id)[:, None, None]
            key_rows = jnp.where(here_mask, fresh_keys, old_keys).reshape(SEQ, HEAD)
            value_rows = jnp.where(here_mask, fresh_values, old_values).reshape(SEQ, HEAD)
            query_rows = lax.dynamic_index_in_dim(query_blocks, block_id, 0, keepdims=False)
            scores = jnp.dot(query_rows, key_rows.T, preferred_element_type=jnp.float32) * score_scale
            scores = jnp.where(live_keys[None, :], scores, -jnp.inf)
            weights_unnorm = jnp.exp(scores - lax.optimization_barrier(jnp.max(scores, axis=1, keepdims=True)))
            weights = weights_unnorm.astype(jnp.bfloat16)
            summed = jnp.dot(weights, value_rows, preferred_element_type=jnp.float32)
            return (summed / lax.optimization_barrier(jnp.sum(weights_unnorm, axis=1, keepdims=True))).astype(jnp.bfloat16)
        return lax.map(one_block, block_ids)
    attended = lax.map(one_head, (by_head(query_rot), by_head(key_rot), by_head(v_fresh), stale_by_head(stale_keys), stale_by_head(stale_values)))
    heads_out = attended.transpose(1, 2, 0, 3).reshape(SEQ, D)
    gate_row = gate_table[timestep[0]].astype(jnp.float32)
    mixed = (heads_out.astype(jnp.float32) * gate_row[None, :]).astype(jnp.bfloat16)
    new_keys = key_rot.reshape(BLOCKS, BLOCK_TOK, GROUPS, HEADS_DEV * HEAD).transpose(0, 2, 1, 3).reshape(N_SEQ, BLOCK_TOK, HEADS_DEV * HEAD)
    new_values = v_fresh.reshape(BLOCKS, BLOCK_TOK, GROUPS, HEADS_DEV * HEAD).transpose(0, 2, 1, 3).reshape(N_SEQ, BLOCK_TOK, HEADS_DEV * HEAD)
    return (mixed, new_keys, new_values)
```

```python
import functools

import jax
import jax.numpy as jnp
import numpy as np
from jax import lax
from jax.experimental import pallas as pl
from jax.experimental.pallas import tpu as pltpu
from jax.sharding import PartitionSpec as P

HEAD = 128
RMS_EPS = 1e-06
VMEM_BYTES = 32 * 1024 * 1024
TILE = 256
SMEM, VMEM = pltpu.SMEM, pltpu.VMEM


def call(kernel, name, ins, outs, flops, n_bytes, scratch=()):
    shapes = [jax.ShapeDtypeStruct(shape, dtype) for _, shape, dtype in outs]
    return pl.pallas_call(
        kernel,
        out_shape=shapes,
        in_specs=[pl.BlockSpec(memory_space=m) for m in ins],
        out_specs=[pl.BlockSpec(memory_space=m) for m, _, _ in outs],
        scratch_shapes=scratch,
        compiler_params=pltpu.CompilerParams(vmem_limit_bytes=VMEM_BYTES),
        cost_estimate=pl.CostEstimate(flops=flops, bytes_accessed=n_bytes, transcendentals=0),
        name=name,
    )


def to_partner(value, distance, size):
    if distance == 0:
        return value
    return lax.ppermute(value, "seq", [(i, i ^ distance) for i in range(size)])


def to_block(value, distance, size):
    return lax.ppermute(value, "seq", [(i, (i + distance) % size) for i in range(size)])


def column(h):
    return slice(h * HEAD, (h + 1) * HEAD)


def place(slots):
    device = lax.axis_index("seq")
    return lax.rem(device, slots), lax.div(device, slots)


def live_of(assign, counts, index):
    return counts[assign[index]]


def live_lanes(assign, counts, tok, indices):
    width = tok * len(indices)
    lane = lax.broadcasted_iota(jnp.int32, (1, width), 1)
    count = jnp.zeros((1, width), jnp.int32)
    for i, index in enumerate(indices):
        count = jnp.where(lane // tok == i, live_of(assign, counts, index), count)
    return lane % tok, count


def compact_kernel(slots, tok, blocks, assign, counts, keys, values, *refs):
    flag, outs = refs[0], refs[1:]
    wide = keys.shape[2]
    rows = slots * tok
    _, block = place(slots)
    indices = [block * slots + i for i in range(slots)]
    within, count = live_lanes(assign, counts, tok, indices)
    lane = lax.broadcasted_iota(jnp.int32, (1, rows), 1)
    ahead = jnp.zeros((1, rows), jnp.int32)
    for i, index in enumerate(indices):
        ahead = ahead + jnp.where(lane // tok > i, live_of(assign, counts, index), 0)
    goal = jnp.where(within < count, ahead + within, -1)
    row = lax.broadcasted_iota(jnp.int32, (rows, rows), 0)
    pick = jnp.where(row == goal, 1.0, 0.0).astype(jnp.bfloat16)
    most = jnp.int32(0)
    for b in range(blocks):
        total = jnp.int32(0)
        for i in range(slots):
            total = total + live_of(assign, counts, b * slots + i)
        most = jnp.maximum(most, total)
    flag[0] = most
    for part, ref in enumerate((keys, values)):
        start = 0
        for out in outs:
            stop = start + out.shape[0]
            moved = jnp.dot(pick[start:stop], ref[0], preferred_element_type=jnp.float32)
            out[:, part * wide : (part + 1) * wide] = moved.astype(jnp.bfloat16)
            start = stop


def norm_kernel(order, heads, assign, q, k, v, q_gain, k_gain, steps, *outs):
    tok, width = q.shape
    slot, block = place(len(order))
    patch = assign[block * len(order) + slot]
    position = patch * tok + lax.broadcasted_iota(jnp.int32, (tok, HEAD), 0)
    angles = position.astype(jnp.float32) * steps[...]
    low = lax.broadcasted_iota(jnp.int32, (tok, HEAD), 1) < HEAD // 2
    cos_part = jnp.cos(angles)
    sin_part = jnp.sin(angles)
    sin_part = jnp.where(low, -sin_part, sin_part)

    def inverse(ref):
        total = jnp.zeros((tok, HEAD), jnp.float32)
        for c in range(0, width, HEAD):
            x = ref[:, c : c + HEAD].astype(jnp.float32)
            total = total + x * x
        return lax.rsqrt(jnp.sum(total, axis=1, keepdims=True) / width + RMS_EPS)

    scales = inverse(q), inverse(k)
    for out, d in zip(outs, order):
        group = jnp.bitwise_xor(slot, d)
        for h in range(heads):
            col = pl.ds(pl.multiple_of((group * heads + h) * HEAD, HEAD), HEAD)
            for part, (ref, gain) in enumerate(((q, q_gain), (k, k_gain))):
                x = ref[:, col].astype(jnp.float32) * scales[part]
                x = x * gain[:, col].astype(jnp.float32)
                turned = x * cos_part + pltpu.roll(x, HEAD // 2, 1) * sin_part
                out[part * tok : (part + 1) * tok, column(h)] = turned.astype(jnp.bfloat16)
            out[2 * tok : 3 * tok, column(h)] = v[:, col]


def cache_kernel(order, tok, *refs):
    new_keys, new_values = refs[len(order) :]
    slot, _ = place(len(order))
    for ref, d in zip(refs, order):
        at = pl.ds(pl.multiple_of(jnp.bitwise_xor(slot, d) * tok, tok), tok)
        new_keys[0, at, :] = ref[tok : 2 * tok, :]
        new_values[0, at, :] = ref[2 * tok : 3 * tok, :]


def softmax_step(queries, keys, values, bias, state):
    scale = HEAD**-0.5
    scores = lax.dot_general(
        queries, keys, (((1,), (1,)), ((), ())), preferred_element_type=jnp.float32
    )
    scores = scores + bias
    top = jnp.max(scores, axis=1, keepdims=True)
    if state is not None:
        top = jnp.maximum(top, state[0])
    weights = jnp.exp((scores - top) * scale)
    total = jnp.sum(weights, axis=1, keepdims=True)
    summed = jnp.dot(weights.astype(jnp.bfloat16), values, preferred_element_type=jnp.float32)
    if state is not None:
        fading = jnp.exp((state[0] - top) * scale)
        total = total + state[1] * fading
        summed = summed + state[2] * fading
    return top, total, summed


def store_state(stats, sums, at, parts):
    rows = parts[0][0].shape[0]
    lane = lax.broadcasted_iota(jnp.int32, (rows, HEAD), 1)
    packed = jnp.zeros((rows, HEAD), jnp.float32)
    for h, (top, total, summed) in enumerate(parts):
        packed = jnp.where(lane == h, top, packed)
        packed = jnp.where(lane == HEAD // 2 + h, total, packed)
        sums[at, column(h)] = summed
    stats[at, :] = packed


def load_state(stats, sums, at, h):
    half = HEAD // 2
    return stats[at, h : h + 1], stats[at, half + h : half + h + 1], sums[at, column(h)]


def fresh_kernel(order, tok, heads, assign, counts, *refs):
    slots = len(order)
    bundles = refs[:slots]
    queries, stats, sums, keys, values = refs[slots:]
    for i, bundle in enumerate(bundles):
        at = slice(i * tok, (i + 1) * tok)
        queries[at, :] = bundle[:tok, :]
        keys[at, :] = bundle[tok : 2 * tok, :]
        values[at, :] = bundle[2 * tok : 3 * tok, :]
    slot, block = place(slots)
    indices = [block * slots + jnp.bitwise_xor(slot, d) for d in order]
    within, count = live_lanes(assign, counts, tok, indices)
    bias = jnp.where(within < count, 0.0, -jnp.inf)
    for start in range(0, slots * tok, TILE):
        at = slice(start, start + TILE)
        parts = []
        for h in range(heads):
            cols = column(h)
            parts.append(
                softmax_step(queries[at, cols], keys[:, cols], values[:, cols], bias, None)
            )
        store_state(stats, sums, at, parts)


def stale_kernel(slots, tok, blocks, step, heads, rows, final, assign, counts, *refs):
    queries, stats, sums = refs[:3]
    pieces = refs[3 : 3 + final[0]]
    rest = refs[3 + final[0] :]
    _, block = place(slots)
    source = lax.rem(block - step + blocks, blocks) * slots
    live = jnp.int32(0)
    for i in range(slots):
        live = live + live_of(assign, counts, source + i)
    width = sum(p.shape[0] for p in pieces)
    lane = lax.broadcasted_iota(jnp.int32, (1, width), 1)
    bias = jnp.where(lane < live, 0.0, -jnp.inf)

    def joined(cols):
        if len(pieces) == 1:
            return pieces[0][:, cols]
        return jnp.concatenate([p[:, cols] for p in pieces], axis=0)

    for start in range(*rows, TILE):
        at = slice(start, start + TILE)
        parts = []
        for h in range(heads):
            parts.append(
                softmax_step(
                    queries[at, column(h)],
                    joined(column(h)),
                    joined(column(heads + h)),
                    bias,
                    load_state(stats, sums, at, h),
                )
            )
        if not final[1]:
            store_state(*rest, at, parts)
            continue
        gate, outs = rest[0], rest[1:]
        for h, (_, total, summed) in enumerate(parts):
            out = (summed / total).astype(jnp.bfloat16).astype(jnp.float32)
            out = (out * gate[:, column(h)].astype(jnp.float32)).astype(jnp.bfloat16)
            for i in range(TILE // tok):
                to = (start - rows[0]) // tok + i
                outs[to][:, column(h)] = out[i * tok : (i + 1) * tok]


def collect_kernel(order, heads, *refs):
    wide = heads * HEAD
    slot, _ = place(len(order))
    for ref, d in zip(refs, order):
        group = jnp.bitwise_xor(slot, d)
        refs[-1][:, pl.ds(pl.multiple_of(group * wide, wide), wide)] = ref[...]


def body(
    q_fresh,
    k_fresh,
    v_fresh,
    q_gain,
    k_gain,
    stale_keys,
    stale_values,
    gate_table,
    assign,
    counts,
    timestep,
):
    bf16, f32, i32 = jnp.bfloat16, jnp.float32, jnp.int32
    device = lax.axis_index("seq")
    size = lax.axis_size("seq")
    tok, model_width = q_fresh.shape
    block_rows, wide = stale_keys.shape[1:]
    slots = model_width // wide
    blocks = size // slots
    heads = wide // HEAD
    order = sorted(range(slots), key=lambda d: (-(d & ~1).bit_count(), -d))
    short = block_rows * 7 // 8 if blocks == 2 else block_rows
    sizes = [n for n in (short, block_rows - short) if n]

    most, *packed = call(
        functools.partial(compact_kernel, slots, tok, blocks),
        "compact",
        [SMEM, SMEM, VMEM, VMEM],
        [(SMEM, (1,), i32)] + [(VMEM, (n, 2 * wide), bf16) for n in sizes],
        4 * block_rows * block_rows * wide,
        8 * block_rows * wide,
    )(assign, counts, stale_keys, stale_values)

    def exchange(arrays, order):
        return [to_partner(a, d, size) for a, d in zip(arrays, order)]

    halves = np.arange(HEAD, dtype=np.float64) % (HEAD // 2)
    steps = jnp.asarray((10000.0 ** (-2.0 * halves / HEAD)).astype(np.float32)[None])

    def run(packed, operands):
        assign, counts, q, k, v, q_gain, k_gain, gate_table, timestep = operands
        stale = [[to_block(p, s * slots, size) for p in packed] for s in range(1, blocks)]
        bundles = call(
            functools.partial(norm_kernel, order, heads),
            "norm",
            [SMEM] + [VMEM] * 6,
            [(VMEM, (3 * tok, wide), bf16)] * slots,
            20 * tok * model_width,
            12 * tok * model_width,
        )(assign, q, k, v, q_gain[None], k_gain[None], steps)
        fresh = exchange(bundles, order)
        gate = lax.dynamic_slice(gate_table, (timestep[0], device % slots * wide), (1, wide))
        state_like = [(VMEM, (block_rows, HEAD), f32), (VMEM, (block_rows, wide), f32)]
        queries, *state = call(
            functools.partial(fresh_kernel, order, tok, heads),
            "fresh",
            [SMEM] * 2 + [VMEM] * slots,
            [(VMEM, (block_rows, wide), bf16), *state_like],
            4 * block_rows * block_rows * wide,
            16 * block_rows * wide,
            [pltpu.VMEM((block_rows, wide), bf16)] * 2,
        )(assign, counts, *fresh)

        def step(s, rows, outs, extra):
            final = (len(packed), s == blocks - 1)
            return call(
                functools.partial(stale_kernel, slots, tok, blocks, s, heads, rows, final),
                "stale",
                [SMEM] * 2 + [VMEM] * (3 + len(packed) + len(extra)),
                outs,
                4 * (rows[1] - rows[0]) * block_rows * wide,
                8 * block_rows * wide,
            )(assign, counts, queries, *state, *stale[s - 1], *extra)

        for s in range(1, blocks - 1):
            state = step(s, (0, block_rows), state_like, [])
        back = []
        for start in range(0, block_rows, TILE):
            part = order[start // tok : (start + TILE) // tok]
            outs = [(VMEM, (tok, wide), bf16)] * len(part)
            back += exchange(step(blocks - 1, (start, start + TILE), outs, [gate]), part)
        new_keys, new_values = call(
            functools.partial(cache_kernel, order, tok),
            "cache",
            [VMEM] * slots,
            [(VMEM, (1, block_rows, wide), bf16)] * 2,
            0,
            8 * block_rows * wide,
        )(*fresh)
        (mixed,) = call(
            functools.partial(collect_kernel, order, heads),
            "collect",
            [VMEM] * slots,
            [(VMEM, (tok, model_width), bf16)],
            0,
            4 * tok * model_width,
        )(*back)
        return mixed, new_keys, new_values

    operands = (
        assign,
        counts,
        q_fresh,
        k_fresh,
        v_fresh,
        q_gain,
        k_gain,
        gate_table,
        timestep,
    )
    if len(sizes) == 1:
        return run(packed, operands)
    return lax.cond(
        most[0] <= sizes[0],
        lambda packed, operands: run(packed[:1], operands),
        run,
        packed,
        operands,
    )


def solution(mesh):
    rows = P(("groups", "seq"), None)
    entries = P(("groups", "seq"), None, None)
    return jax.shard_map(
        body,
        mesh=mesh,
        in_specs=(
            rows,
            rows,
            rows,
            P(),
            P(),
            entries,
            entries,
            P(),
            P("groups"),
            P("groups"),
            P("groups"),
        ),
        out_specs=(rows, entries, entries),
        check_vma=False,
    )
```

```python
import functools
import math

import jax
import jax.numpy as jnp
import numpy as np
from jax import lax
from jax.experimental import pallas as pl
from jax.experimental.pallas import tpu as pltpu
from jax.sharding import PartitionSpec as P

HEAD = 128
RMS_EPS = 1e-06
VMEM_BYTES = 32 * 1024 * 1024
TILE = 512
SMEM, VMEM = pltpu.SMEM, pltpu.VMEM


def call(kernel, name, ins, outs, flops, n_bytes, scratch=(), vmem_bytes=VMEM_BYTES):
    shapes = [jax.ShapeDtypeStruct(shape, dtype) for _, shape, dtype in outs]
    return pl.pallas_call(
        kernel,
        out_shape=shapes,
        in_specs=[pl.BlockSpec(memory_space=m) for m in ins],
        out_specs=[pl.BlockSpec(memory_space=m) for m, _, _ in outs],
        scratch_shapes=scratch,
        compiler_params=pltpu.CompilerParams(vmem_limit_bytes=vmem_bytes),
        cost_estimate=pl.CostEstimate(flops=flops, bytes_accessed=n_bytes, transcendentals=0),
        name=name,
    )


def to_partner(value, distance, size):
    if distance == 0:
        return value
    return lax.ppermute(value, "seq", [(i, i ^ distance) for i in range(size)])


def to_block(value, distance, size):
    return lax.ppermute(value, "seq", [(i, (i + distance) % size) for i in range(size)])


def column(h):
    return slice(h * HEAD, (h + 1) * HEAD)


def place(slots):
    device = lax.axis_index("seq")
    return lax.rem(device, slots), lax.div(device, slots)


def live_of(assign, counts, index):
    return counts[assign[index]]


def live_lanes(assign, counts, tok, indices):
    width = tok * len(indices)
    lane = lax.broadcasted_iota(jnp.int32, (1, width), 1)
    count = jnp.zeros((1, width), jnp.int32)
    for i, index in enumerate(indices):
        count = jnp.where(lane // tok == i, live_of(assign, counts, index), count)
    return lane % tok, count


def most_kernel(slots, blocks, assign, counts, out):
    most = jnp.int32(0)
    for b in range(blocks):
        total = jnp.int32(0)
        for i in range(slots):
            total = total + live_of(assign, counts, b * slots + i)
        most = jnp.maximum(most, total)
    out[0] = most


def compact_kernel(slots, tok, assign, counts, keys, values, out):
    rows, width, wide = out.shape[0], slots * tok, keys.shape[2]
    _, block = place(slots)
    indices = [block * slots + i for i in range(slots)]
    within, count = live_lanes(assign, counts, tok, indices)
    lane = lax.broadcasted_iota(jnp.int32, (1, width), 1)
    ahead = jnp.zeros((1, width), jnp.int32)
    for i, index in enumerate(indices):
        ahead = ahead + jnp.where(lane // tok > i, live_of(assign, counts, index), 0)
    goal = jnp.where(within < count, ahead + within, -1)
    row = lax.broadcasted_iota(jnp.int32, (rows, width), 0)
    pick = jnp.where(row == goal, 1.0, 0.0).astype(jnp.bfloat16)
    for part, ref in enumerate((keys, values)):
        moved = jnp.dot(pick, ref[0], preferred_element_type=jnp.float32)
        out[:, part * wide : (part + 1) * wide] = moved.astype(jnp.bfloat16)


def norm_kernel(order, heads, assign, q, k, v, q_gain, k_gain, steps, *outs):
    tok, width = q.shape
    slot, block = place(len(order))
    patch = assign[block * len(order) + slot]
    position = patch * tok + lax.broadcasted_iota(jnp.int32, (tok, HEAD), 0)
    angles = position.astype(jnp.float32) * steps[...]
    low = lax.broadcasted_iota(jnp.int32, (tok, HEAD), 1) < HEAD // 2
    cos_part = jnp.cos(angles)
    sin_part = jnp.sin(angles)
    sin_part = jnp.where(low, -sin_part, sin_part)

    def inverse(ref):
        total = jnp.zeros((tok, HEAD), jnp.float32)
        for c in range(0, width, HEAD):
            x = ref[:, c : c + HEAD].astype(jnp.float32)
            total = total + x * x
        return lax.rsqrt(jnp.sum(total, axis=1, keepdims=True) / width + RMS_EPS)

    scales = inverse(q), inverse(k)
    wide = heads * HEAD
    for out, d in zip(outs, order):
        cols = pl.ds(pl.multiple_of(jnp.bitwise_xor(slot, d) * wide, wide), wide)
        out[2 * tok : 3 * tok, :] = v[:, cols]
        for part, (ref, gain) in enumerate(((q, q_gain), (k, k_gain))):
            entries, gains = ref[:, cols], gain[:, cols]
            for h in range(heads):
                x = entries[:, column(h)].astype(jnp.float32) * scales[part]
                x = x * gains[:, column(h)].astype(jnp.float32)
                turned = x * cos_part + pltpu.roll(x, HEAD // 2, 1) * sin_part
                out[part * tok : (part + 1) * tok, column(h)] = turned.astype(jnp.bfloat16)


def cache_kernel(order, tok, *refs):
    new_keys, new_values = refs[len(order) :]
    slot, _ = place(len(order))
    for ref, d in zip(refs, order):
        at = pl.ds(pl.multiple_of(jnp.bitwise_xor(slot, d) * tok, tok), tok)
        new_keys[0, at, :] = ref[tok : 2 * tok, :]
        new_values[0, at, :] = ref[2 * tok : 3 * tok, :]


def attend(queries, sources, state):
    scale = HEAD**-0.5 / math.log(2.0)
    scores = [
        lax.dot_general(
            queries, keys, (((1,), (1,)), ((), ())), preferred_element_type=jnp.float32
        )
        + bias
        for keys, _, bias in sources
    ]
    tops = [jnp.max(s, axis=1, keepdims=True) for s in scores]
    top = functools.reduce(jnp.maximum, tops + ([] if state is None else [state[0]]))
    weights = [jnp.exp2(s * scale - top * scale) for s in scores]
    total = sum(jnp.sum(w, axis=1, keepdims=True) for w in weights)
    summed = sum(
        jnp.dot(w.astype(jnp.bfloat16), values, preferred_element_type=jnp.float32)
        for w, (_, values, _) in zip(weights, sources)
    )
    if state is not None:
        fading = jnp.exp2((state[0] - top) * scale)
        total = total + state[1] * fading
        summed = summed + state[2] * fading
    return top, total, summed


def store_state(stats, sums, at, parts):
    rows = parts[0][0].shape[0]
    lane = lax.broadcasted_iota(jnp.int32, (rows, HEAD), 1)
    packed = jnp.zeros((rows, HEAD), jnp.float32)
    for h, (top, total, summed) in enumerate(parts):
        packed = jnp.where(lane == h, top, packed)
        packed = jnp.where(lane == HEAD // 2 + h, total, packed)
        sums[at, column(h)] = summed
    stats[at, :] = packed


def load_state(stats, sums, at, h):
    half = HEAD // 2
    return stats[at, h : h + 1], stats[at, half + h : half + h + 1], sums[at, column(h)]


def attend_kernel(order, tok, blocks, heads, rows, step, n_state, assign, counts, *refs):
    slots = len(order)
    bundles, refs = refs[:slots], refs[slots:]
    stale, state, rest = refs[0], refs[1 : 1 + n_state], refs[1 + n_state :]
    final = step == blocks - 1
    slot, block = place(slots)
    source = lax.rem(block - step + blocks, blocks) * slots
    live = jnp.int32(0)
    for i in range(slots):
        live = live + live_of(assign, counts, source + i)
    lane = lax.broadcasted_iota(jnp.int32, (1, stale.shape[0]), 1)
    stale_bias = jnp.where(lane < live, 0.0, -jnp.inf)
    if final:
        rest[-(rows[1] - rows[0]) // tok - 1][...] = jnp.zeros((8, HEAD), jnp.float32)
        gate, outs = rest[0], rest[-(rows[1] - rows[0]) // tok :]
        indices = [block * slots + jnp.bitwise_xor(slot, d) for d in order]
        within, count = live_lanes(assign, counts, tok, indices)
        fresh_bias = jnp.where(within < count, 0.0, -jnp.inf)

    def fresh(part, first, last, cols):
        rows = [bundles[i][part * tok : (part + 1) * tok, cols] for i in range(first, last)]
        return jnp.concatenate(rows, axis=0)

    per_tile = min(TILE, rows[1] - rows[0]) // tok
    for first in range(rows[0] // tok, rows[1] // tok, per_tile):
        at = slice(first * tok, (first + per_tile) * tok)
        parts = []
        for h in range(heads):
            cols = column(h)
            sources = [(stale[:, cols], stale[:, column(heads + h)], stale_bias)]
            if final:
                keys, values = fresh(1, 0, slots, cols), fresh(2, 0, slots, cols)
                sources.append((keys, values, fresh_bias))
            before = load_state(*state, at, h) if state else None
            _, total, summed = result = attend(
                fresh(0, first, first + per_tile, cols), sources, before
            )
            parts.append(result)
            if final:
                rounded = (summed / total).astype(jnp.bfloat16).astype(jnp.float32)
                gated = (rounded * gate[:, cols].astype(jnp.float32)).astype(jnp.bfloat16)
                for i in range(per_tile):
                    to = first + i - rows[0] // tok
                    outs[to][:, cols] = gated[i * tok : (i + 1) * tok]
        if not final:
            store_state(*rest, at, parts)


def collect_kernel(order, heads, *refs):
    wide = heads * HEAD
    slot, _ = place(len(order))
    for ref, d in zip(refs, order):
        start = jnp.bitwise_xor(slot, d) * wide
        refs[-1][:, pl.ds(pl.multiple_of(start, wide), wide)] = ref[...]


def body(
    q_fresh,
    k_fresh,
    v_fresh,
    q_gain,
    k_gain,
    stale_keys,
    stale_values,
    gate_table,
    assign,
    counts,
    timestep,
):
    bf16, f32, i32 = jnp.bfloat16, jnp.float32, jnp.int32
    device = lax.axis_index("seq")
    size = lax.axis_size("seq")
    tok, model_width = q_fresh.shape
    block_rows, wide = stale_keys.shape[1:]
    slots = model_width // wide
    blocks = size // slots
    heads = wide // HEAD
    order = sorted(range(slots), key=lambda d: (-(d & ~1).bit_count(), -d))
    sizes = [block_rows * n // 32 for n in (26, 28, 32)] if blocks == 2 else [block_rows]

    (most,) = call(
        functools.partial(most_kernel, slots, blocks),
        "most",
        [SMEM] * 2,
        [(SMEM, (1,), i32)],
        0,
        8 * (block_rows * wide + tok * model_width),
    )(assign, counts)

    halves = np.arange(HEAD, dtype=np.float64) % (HEAD // 2)
    steps = jnp.asarray((10000.0 ** (-2.0 * halves / HEAD)).astype(np.float32)[None])

    def exchange(arrays, order):
        return [to_partner(a, d, size) for a, d in zip(arrays, order)]

    def run(rows, operands):
        assign, counts, keys, values, q, k, v, q_gain, k_gain, gate_table, timestep = operands
        (packed,) = call(
            functools.partial(compact_kernel, slots, tok),
            "compact",
            [SMEM] * 2 + [VMEM] * 2,
            [(VMEM, (rows, 2 * wide), bf16)],
            4 * rows * block_rows * wide,
            4 * (rows + block_rows) * wide,
        )(assign, counts, keys, values)
        stale = [to_block(packed, s * slots, size) for s in range(1, blocks)]
        bundles = call(
            functools.partial(norm_kernel, order, heads),
            "norm",
            [SMEM] + [VMEM] * 6,
            [(VMEM, (3 * tok, wide), bf16)] * slots,
            20 * tok * model_width,
            12 * tok * model_width,
        )(assign, q, k, v, q_gain[None], k_gain[None], steps)
        fresh = exchange(bundles, order)
        gate = lax.dynamic_slice(gate_table, (timestep[0], device % slots * wide), (1, wide))
        state, back = [], []

        def step(s, rows, outs, extra):
            given = [*fresh, stale[s - 1], *state, *extra]
            return call(
                functools.partial(
                    attend_kernel, order, tok, blocks, heads, rows, s, len(state)
                ),
                "attend",
                [SMEM] * 2 + [VMEM] * len(given),
                outs,
                8 * (rows[1] - rows[0]) * block_rows * wide,
                16 * block_rows * wide,
            )(assign, counts, *given)

        for s in range(1, blocks - 1):
            state = step(
                s, (0, block_rows), [(VMEM, (block_rows, n), f32) for n in (HEAD, wide)], []
            )
        extra, start = [gate], 0
        for n in (slots,):
            part = order[start : start + n]
            outs = [(VMEM, (8, HEAD), f32)] + [(VMEM, (tok, wide), bf16)] * n
            ends = (start * tok, (start + n) * tok)
            after, *outs = step(blocks - 1, ends, outs, extra)
            extra, start = [gate, after], start + n
            back += exchange(outs, part)
        new_keys, new_values = call(
            functools.partial(cache_kernel, order, tok),
            "cache",
            [VMEM] * slots,
            [(VMEM, (1, block_rows, wide), bf16)] * 2,
            0,
            8 * block_rows * wide,
        )(*fresh)
        (mixed,) = call(
            functools.partial(collect_kernel, order, heads),
            "collect",
            [VMEM] * len(back),
            [(VMEM, (tok, model_width), bf16)],
            0,
            4 * tok * model_width,
        )(*back)
        return mixed, new_keys, new_values

    operands = (
        assign,
        counts,
        stale_keys,
        stale_values,
        q_fresh,
        k_fresh,
        v_fresh,
        q_gain,
        k_gain,
        gate_table,
        timestep,
    )
    which = sum((most[0] > n).astype(i32) for n in sizes[:-1])
    return lax.switch(which, [functools.partial(run, rows) for rows in sizes], operands)


def solution(mesh):
    rows = P(("groups", "seq"), None)
    entries = P(("groups", "seq"), None, None)
    return jax.shard_map(
        body,
        mesh=mesh,
        in_specs=(
            rows,
            rows,
            rows,
            P(),
            P(),
            entries,
            entries,
            P(),
            P("groups"),
            P("groups"),
            P("groups"),
        ),
        out_specs=(rows, entries, entries),
        check_vma=False,
    )
```

```python
import functools
import math

import jax
import jax.numpy as jnp
import numpy as np
from jax import lax
from jax.experimental import pallas as pl
from jax.experimental.pallas import tpu as pltpu
from jax.sharding import PartitionSpec as P

HEAD = 128
RMS_EPS = 1e-06
VMEM_BYTES = 32 * 1024 * 1024
TILE = 512
SMEM, VMEM = pltpu.SMEM, pltpu.VMEM


def call(kernel, name, ins, outs, flops, n_bytes, scratch=()):
    shapes = [jax.ShapeDtypeStruct(shape, dtype) for _, shape, dtype in outs]
    return pl.pallas_call(
        kernel,
        out_shape=shapes,
        in_specs=[pl.BlockSpec(memory_space=m) for m in ins],
        out_specs=[pl.BlockSpec(memory_space=m) for m, _, _ in outs],
        scratch_shapes=scratch,
        compiler_params=pltpu.CompilerParams(vmem_limit_bytes=VMEM_BYTES),
        cost_estimate=pl.CostEstimate(flops=flops, bytes_accessed=n_bytes, transcendentals=0),
        name=name,
    )


def to_partner(value, distance, size):
    if distance == 0:
        return value
    return lax.ppermute(value, "seq", [(i, i ^ distance) for i in range(size)])


def to_block(value, distance, size):
    return lax.ppermute(value, "seq", [(i, (i + distance) % size) for i in range(size)])


def column(h):
    return slice(h * HEAD, (h + 1) * HEAD)


def place(slots):
    device = lax.axis_index("seq")
    return lax.rem(device, slots), lax.div(device, slots)


def live_of(assign, counts, index):
    return counts[assign[index]]


def live_lanes(assign, counts, tok, indices):
    width = tok * len(indices)
    lane = lax.broadcasted_iota(jnp.int32, (1, width), 1)
    count = jnp.zeros((1, width), jnp.int32)
    for i, index in enumerate(indices):
        count = jnp.where(lane // tok == i, live_of(assign, counts, index), count)
    return lane % tok, count


def choose_kernel(slots, blocks, sizes, assign, counts, out):
    most = jnp.int32(0)
    for b in range(blocks):
        total = jnp.int32(0)
        for i in range(slots):
            total = total + live_of(assign, counts, b * slots + i)
        most = jnp.maximum(most, total)
    which = jnp.int32(0)
    for n in sizes[:-1]:
        which = which + (most > n).astype(jnp.int32)
    out[0] = which


def compact_kernel(slots, tok, assign, counts, keys, values, out):
    rows, width, wide = out.shape[0], slots * tok, keys.shape[2]
    _, block = place(slots)
    indices = [block * slots + i for i in range(slots)]
    within, count = live_lanes(assign, counts, tok, indices)
    lane = lax.broadcasted_iota(jnp.int32, (1, width), 1)
    ahead = jnp.zeros((1, width), jnp.int32)
    for i, index in enumerate(indices):
        ahead = ahead + jnp.where(lane // tok > i, live_of(assign, counts, index), 0)
    goal = jnp.where(within < count, ahead + within, -1)
    row = lax.broadcasted_iota(jnp.int32, (rows, width), 0)
    pick = jnp.where(row == goal, 1.0, 0.0).astype(jnp.bfloat16)
    for part, ref in enumerate((keys, values)):
        moved = jnp.dot(pick, ref[0], preferred_element_type=jnp.float32)
        out[:, part * wide : (part + 1) * wide] = moved.astype(jnp.bfloat16)


def norm_kernel(slots, order, heads, assign, q, k, v, q_gain, k_gain, steps, *outs):
    tok, width = q.shape
    slot, block = place(slots)
    patch = assign[block * slots + slot]
    position = patch * tok + lax.broadcasted_iota(jnp.int32, (tok, HEAD), 0)
    angles = position.astype(jnp.float32) * steps[...]
    low = lax.broadcasted_iota(jnp.int32, (tok, HEAD), 1) < HEAD // 2
    cos_part = jnp.cos(angles)
    sin_part = jnp.sin(angles)
    sin_part = jnp.where(low, -sin_part, sin_part)

    def inverse(ref):
        total = jnp.zeros((tok, HEAD), jnp.float32)
        for c in range(0, width, HEAD):
            x = ref[:, c : c + HEAD].astype(jnp.float32)
            total = total + x * x
        return lax.rsqrt(jnp.sum(total, axis=1, keepdims=True) / width + RMS_EPS)

    scales = inverse(q), inverse(k)
    wide = heads * HEAD
    for out, d in zip(outs, order):
        cols = pl.ds(pl.multiple_of(jnp.bitwise_xor(slot, d) * wide, wide), wide)
        out[2 * tok : 3 * tok, :] = v[:, cols]
        for part, (ref, gain) in enumerate(((q, q_gain), (k, k_gain))):
            entries, gains = ref[:, cols], gain[:, cols]
            for h in range(heads):
                x = entries[:, column(h)].astype(jnp.float32) * scales[part]
                x = x * gains[:, column(h)].astype(jnp.float32)
                turned = x * cos_part + pltpu.roll(x, HEAD // 2, 1) * sin_part
                out[part * tok : (part + 1) * tok, column(h)] = turned.astype(jnp.bfloat16)


def cache_kernel(order, tok, *refs):
    new_keys, new_values = refs[len(order) :]
    slot, _ = place(len(order))
    for ref, d in zip(refs, order):
        at = pl.ds(pl.multiple_of(jnp.bitwise_xor(slot, d) * tok, tok), tok)
        new_keys[0, at, :] = ref[tok : 2 * tok, :]
        new_values[0, at, :] = ref[2 * tok : 3 * tok, :]


def attend(queries, sources, state):
    scale = HEAD**-0.5 / math.log(2.0)
    scores = [
        lax.dot_general(
            queries, keys, (((1,), (1,)), ((), ())), preferred_element_type=jnp.float32
        )
        + bias
        for keys, _, bias in sources
    ]
    tops = [jnp.max(s, axis=1, keepdims=True) for s in scores]
    top = functools.reduce(jnp.maximum, tops + ([] if state is None else [state[0]]))
    weights = [jnp.exp2(s * scale - top * scale) for s in scores]
    total = sum(jnp.sum(w, axis=1, keepdims=True) for w in weights)
    summed = sum(
        jnp.dot(w.astype(jnp.bfloat16), values, preferred_element_type=jnp.float32)
        for w, (_, values, _) in zip(weights, sources)
    )
    if state is not None:
        fading = jnp.exp2((state[0] - top) * scale)
        total = total + state[1] * fading
        summed = summed + state[2] * fading
    return top, total, summed


def store_state(stats, sums, at, parts):
    rows = parts[0][0].shape[0]
    lane = lax.broadcasted_iota(jnp.int32, (rows, HEAD), 1)
    packed = jnp.zeros((rows, HEAD), jnp.float32)
    for h, (top, total, summed) in enumerate(parts):
        packed = jnp.where(lane == h, top, packed)
        packed = jnp.where(lane == HEAD // 2 + h, total, packed)
        sums[at, column(h)] = summed
    stats[at, :] = packed


def load_state(stats, sums, at, h):
    half = HEAD // 2
    return stats[at, h : h + 1], stats[at, half + h : half + h + 1], sums[at, column(h)]


def attend_kernel(order, tok, blocks, heads, rows, step, n_state, assign, counts, *refs):
    slots = len(order)
    bundles, refs = refs[:slots], refs[slots:]
    stale, state, rest = refs[0], refs[1 : 1 + n_state], refs[1 + n_state :]
    final = step == blocks - 1
    slot, block = place(slots)
    source = lax.rem(block - step + blocks, blocks) * slots
    live = jnp.int32(0)
    for i in range(slots):
        live = live + live_of(assign, counts, source + i)
    lane = lax.broadcasted_iota(jnp.int32, (1, stale.shape[0]), 1)
    stale_bias = jnp.where(lane < live, 0.0, -jnp.inf)
    if final:
        gate, outs = rest[0], rest[-(rows[1] - rows[0]) // tok :]
        indices = [block * slots + jnp.bitwise_xor(slot, d) for d in order]
        within, count = live_lanes(assign, counts, tok, indices)
        fresh_bias = jnp.where(within < count, 0.0, -jnp.inf)

    def fresh(part, first, last, cols):
        rows = [bundles[i][part * tok : (part + 1) * tok, cols] for i in range(first, last)]
        return jnp.concatenate(rows, axis=0)

    per_tile = min(TILE, rows[1] - rows[0]) // tok
    for first in range(rows[0] // tok, rows[1] // tok, per_tile):
        at = slice(first * tok, (first + per_tile) * tok)
        parts = []
        for h in range(heads):
            cols = column(h)
            sources = [(stale[:, cols], stale[:, column(heads + h)], stale_bias)]
            if final:
                keys, values = fresh(1, 0, slots, cols), fresh(2, 0, slots, cols)
                sources.append((keys, values, fresh_bias))
            before = load_state(*state, at, h) if state else None
            _, total, summed = result = attend(
                fresh(0, first, first + per_tile, cols), sources, before
            )
            parts.append(result)
            if final:
                rounded = (summed / total).astype(jnp.bfloat16).astype(jnp.float32)
                gated = (rounded * gate[:, cols].astype(jnp.float32)).astype(jnp.bfloat16)
                for i in range(per_tile):
                    to = first + i - rows[0] // tok
                    outs[to][:, cols] = gated[i * tok : (i + 1) * tok]
        if not final:
            store_state(*rest, at, parts)


def collect_kernel(order, heads, *refs):
    wide = heads * HEAD
    slot, _ = place(len(order))
    for ref, d in zip(refs, order):
        start = jnp.bitwise_xor(slot, d) * wide
        refs[-1][:, pl.ds(pl.multiple_of(start, wide), wide)] = ref[...]


def body(
    q_fresh,
    k_fresh,
    v_fresh,
    q_gain,
    k_gain,
    stale_keys,
    stale_values,
    gate_table,
    assign,
    counts,
    timestep,
):
    bf16, f32, i32 = jnp.bfloat16, jnp.float32, jnp.int32
    device = lax.axis_index("seq")
    size = lax.axis_size("seq")
    tok, model_width = q_fresh.shape
    block_rows, wide = stale_keys.shape[1:]
    slots = model_width // wide
    blocks = size // slots
    heads = wide // HEAD
    order = [6, 4, 7, 5, 2, 3, 1, 0]
    back_order = [3, 1, 6, 7, 4, 5, 2, 0]
    sizes = [block_rows * n // 32 for n in (26, 28, 32)] if blocks == 2 else [block_rows]

    (which,) = call(
        functools.partial(choose_kernel, slots, blocks, sizes),
        "choose",
        [SMEM] * 2,
        [(SMEM, (1,), i32)],
        0,
        8 * (block_rows * wide + tok * model_width),
    )(assign, counts)

    halves = np.arange(HEAD, dtype=np.float64) % (HEAD // 2)
    steps = jnp.asarray((10000.0 ** (-2.0 * halves / HEAD)).astype(np.float32)[None])

    def exchange(arrays, order):
        return [to_partner(a, d, size) for a, d in zip(arrays, order)]

    def run(rows, operands):
        assign, counts, keys, values, q, k, v, q_gain, k_gain, gate_table, timestep = operands
        (packed,) = call(
            functools.partial(compact_kernel, slots, tok),
            "compact",
            [SMEM] * 2 + [VMEM] * 2,
            [(VMEM, (rows, 2 * wide), bf16)],
            4 * rows * block_rows * wide,
            4 * (rows + block_rows) * wide,
        )(assign, counts, keys, values)
        stale = [to_block(packed, s * slots, size) for s in range(1, blocks)]
        bundles = []
        for part in (order[: slots // 2], order[slots // 2 :]):
            bundles += call(
                functools.partial(norm_kernel, slots, part, heads),
                "norm",
                [SMEM] + [VMEM] * 6,
                [(VMEM, (3 * tok, wide), bf16)] * len(part),
                12 * tok * model_width,
                8 * tok * model_width,
            )(assign, q, k, v, q_gain[None], k_gain[None], steps)
        fresh = exchange(bundles, order)
        gate = lax.dynamic_slice(gate_table, (timestep[0], device % slots * wide), (1, wide))
        state = []

        def step(s, rows, outs, extra):
            given = [*fresh, stale[s - 1], *state, *extra]
            return call(
                functools.partial(
                    attend_kernel, order, tok, blocks, heads, rows, s, len(state)
                ),
                "attend",
                [SMEM] * 2 + [VMEM] * len(given),
                outs,
                8 * (rows[1] - rows[0]) * block_rows * wide,
                16 * block_rows * wide,
            )(assign, counts, *given)

        for s in range(1, blocks - 1):
            state = step(
                s, (0, block_rows), [(VMEM, (block_rows, n), f32) for n in (HEAD, wide)], []
            )
        outs = step(blocks - 1, (0, block_rows), [(VMEM, (tok, wide), bf16)] * slots, [gate])
        back = exchange([outs[order.index(d)] for d in back_order], back_order)
        new_keys, new_values = call(
            functools.partial(cache_kernel, order, tok),
            "cache",
            [VMEM] * slots,
            [(VMEM, (1, block_rows, wide), bf16)] * 2,
            0,
            8 * block_rows * wide,
        )(*fresh)
        (mixed,) = call(
            functools.partial(collect_kernel, back_order, heads),
            "collect",
            [VMEM] * len(back),
            [(VMEM, (tok, model_width), bf16)],
            0,
            4 * tok * model_width,
        )(*back)
        return mixed, new_keys, new_values

    operands = (
        assign,
        counts,
        stale_keys,
        stale_values,
        q_fresh,
        k_fresh,
        v_fresh,
        q_gain,
        k_gain,
        gate_table,
        timestep,
    )
    return lax.switch(which[0], [functools.partial(run, rows) for rows in sizes], operands)


def solution(mesh):
    rows = P(("groups", "seq"), None)
    entries = P(("groups", "seq"), None, None)
    return jax.shard_map(
        body,
        mesh=mesh,
        in_specs=(
            rows,
            rows,
            rows,
            P(),
            P(),
            entries,
            entries,
            P(),
            P("groups"),
            P("groups"),
            P("groups"),
        ),
        out_specs=(rows, entries, entries),
        check_vma=False,
    )
```

```python
import functools
import math

import jax
import jax.numpy as jnp
import numpy as np
from jax import lax
from jax.experimental import pallas as pl
from jax.experimental.pallas import tpu as pltpu
from jax.sharding import PartitionSpec as P

HEAD = 128
RMS_EPS = 1e-06
VMEM_BYTES = 32 * 1024 * 1024
SMEM, VMEM = pltpu.SMEM, pltpu.VMEM


def call(kernel, name, ins, outs, flops, n_bytes, scratch=()):
    shapes = [jax.ShapeDtypeStruct(shape, dtype) for _, shape, dtype in outs]
    return pl.pallas_call(
        kernel,
        out_shape=shapes,
        in_specs=[pl.BlockSpec(memory_space=m) for m in ins],
        out_specs=[pl.BlockSpec(memory_space=m) for m, _, _ in outs],
        scratch_shapes=scratch,
        compiler_params=pltpu.CompilerParams(vmem_limit_bytes=VMEM_BYTES),
        cost_estimate=pl.CostEstimate(flops=flops, bytes_accessed=n_bytes, transcendentals=0),
        name=name,
    )


def to_partner(value, distance, size):
    if distance == 0:
        return value
    return lax.ppermute(value, "seq", [(i, i ^ distance) for i in range(size)])


def to_block(value, distance, size):
    return lax.ppermute(value, "seq", [(i, (i + distance) % size) for i in range(size)])


def column(h):
    return slice(h * HEAD, (h + 1) * HEAD)


def place(slots):
    device = lax.axis_index("seq")
    return lax.rem(device, slots), lax.div(device, slots)


def live_of(assign, counts, index):
    return counts[assign[index]]


def live_lanes(assign, counts, tok, indices):
    width = tok * len(indices)
    lane = lax.broadcasted_iota(jnp.int32, (1, width), 1)
    count = jnp.zeros((1, width), jnp.int32)
    for i, index in enumerate(indices):
        count = jnp.where(lane // tok == i, live_of(assign, counts, index), count)
    return lane % tok, count


def choose_kernel(slots, blocks, sizes, assign, counts, out):
    most = jnp.int32(0)
    for b in range(blocks):
        total = jnp.int32(0)
        for i in range(slots):
            total = total + live_of(assign, counts, b * slots + i)
        most = jnp.maximum(most, total)
    which = jnp.int32(0)
    for n in sizes[:-1]:
        which = which + (most > n).astype(jnp.int32)
    out[0] = which


def compact_kernel(slots, tok, assign, counts, keys, values, out):
    rows, width, wide = out.shape[0], slots * tok, keys.shape[2]
    _, block = place(slots)
    indices = [block * slots + i for i in range(slots)]
    within, count = live_lanes(assign, counts, tok, indices)
    lane = lax.broadcasted_iota(jnp.int32, (1, width), 1)
    ahead = jnp.zeros((1, width), jnp.int32)
    for i, index in enumerate(indices):
        ahead = ahead + jnp.where(lane // tok > i, live_of(assign, counts, index), 0)
    goal = jnp.where(within < count, ahead + within, -1)
    row = lax.broadcasted_iota(jnp.int32, (rows, width), 0)
    pick = jnp.where(row == goal, 1.0, 0.0).astype(jnp.bfloat16)
    for part, ref in enumerate((keys, values)):
        moved = jnp.dot(pick, ref[0], preferred_element_type=jnp.float32)
        out[:, part * wide : (part + 1) * wide] = moved.astype(jnp.bfloat16)


def norm_kernel(slots, order, heads, assign, q, k, v, q_gain, k_gain, steps, *outs):
    tok, width = q.shape
    slot, block = place(slots)
    patch = assign[block * slots + slot]
    position = patch * tok + lax.broadcasted_iota(jnp.int32, (tok, HEAD), 0)
    angles = position.astype(jnp.float32) * steps[...]
    low = lax.broadcasted_iota(jnp.int32, (tok, HEAD), 1) < HEAD // 2
    cos_part = jnp.cos(angles)
    sin_part = jnp.sin(angles)
    sin_part = jnp.where(low, -sin_part, sin_part)

    def inverse(ref):
        total = jnp.zeros((tok, HEAD), jnp.float32)
        for c in range(0, width, HEAD):
            x = ref[:, c : c + HEAD].astype(jnp.float32)
            total = total + x * x
        return lax.rsqrt(jnp.sum(total, axis=1, keepdims=True) / width + RMS_EPS)

    scales = inverse(q), inverse(k)
    wide = heads * HEAD

    def one_head(h, _):
        to = pl.ds(pl.multiple_of(h * HEAD, HEAD), HEAD)
        for out, d in zip(outs, order):
            start = jnp.bitwise_xor(slot, d) * wide + h * HEAD
            col = pl.ds(pl.multiple_of(start, HEAD), HEAD)
            out[2 * tok : 3 * tok, to] = v[:, col]
            for part, (ref, gain) in enumerate(((q, q_gain), (k, k_gain))):
                x = ref[:, col].astype(jnp.float32) * scales[part]
                x = x * gain[:, col].astype(jnp.float32)
                turned = x * cos_part + pltpu.roll(x, HEAD // 2, 1) * sin_part
                out[part * tok : (part + 1) * tok, to] = turned.astype(jnp.bfloat16)
        return 0

    lax.fori_loop(0, heads, one_head, 0)


def cache_kernel(order, tok, *refs):
    new_keys, new_values = refs[len(order) :]
    slot, _ = place(len(order))
    for ref, d in zip(refs, order):
        at = pl.ds(pl.multiple_of(jnp.bitwise_xor(slot, d) * tok, tok), tok)
        new_keys[0, at, :] = ref[tok : 2 * tok, :]
        new_values[0, at, :] = ref[2 * tok : 3 * tok, :]


def attend(queries, sources, state):
    scale = HEAD**-0.5 / math.log(2.0)
    scores = [
        lax.dot_general(
            queries, keys, (((1,), (1,)), ((), ())), preferred_element_type=jnp.float32
        )
        + bias
        for keys, _, bias in sources
    ]
    tops = [jnp.max(s, axis=1, keepdims=True) for s in scores]
    top = functools.reduce(jnp.maximum, tops + ([] if state is None else [state[0]]))
    weights = [jnp.exp2(s * scale - top * scale) for s in scores]
    total = sum(jnp.sum(w, axis=1, keepdims=True) for w in weights)
    summed = sum(
        jnp.dot(w.astype(jnp.bfloat16), values, preferred_element_type=jnp.float32)
        for w, (_, values, _) in zip(weights, sources)
    )
    if state is not None:
        fading = jnp.exp2((state[0] - top) * scale)
        total = total + state[1] * fading
        summed = summed + state[2] * fading
    return top, total, summed


def store_state(stats, sums, parts):
    rows = parts[0][0].shape[0]
    lane = lax.broadcasted_iota(jnp.int32, (rows, HEAD), 1)
    packed = jnp.zeros((rows, HEAD), jnp.float32)
    for h, (top, total, summed) in enumerate(parts):
        packed = jnp.where(lane == h, top, packed)
        packed = jnp.where(lane == HEAD // 2 + h, total, packed)
        sums[:, column(h)] = summed
    stats[...] = packed


def load_state(stats, sums, h):
    half = HEAD // 2
    return stats[:, h : h + 1], stats[:, half + h : half + h + 1], sums[:, column(h)]


def attend_kernel(order, tok, blocks, heads, looped, step, n_state, assign, counts, *refs):
    slots = len(order)
    bundles, refs = refs[:slots], refs[slots:]
    stale, state, rest = refs[0], refs[1 : 1 + n_state], refs[1 + n_state :]
    final = step == blocks - 1
    slot, block = place(slots)
    source = lax.rem(block - step + blocks, blocks) * slots
    live = jnp.int32(0)
    for i in range(slots):
        live = live + live_of(assign, counts, source + i)
    lane = lax.broadcasted_iota(jnp.int32, (1, stale.shape[0]), 1)
    stale_bias = jnp.where(lane < live, 0.0, -jnp.inf)
    if final:
        gate, outs = rest[0], rest[1:]
        indices = [block * slots + jnp.bitwise_xor(slot, d) for d in order]
        within, count = live_lanes(assign, counts, tok, indices)
        fresh_bias = jnp.where(within < count, 0.0, -jnp.inf)

    def fresh(part, cols):
        return jnp.concatenate([r[part * tok : (part + 1) * tok, cols] for r in bundles], axis=0)

    def one_head(h):
        cols, past = [
            pl.ds(pl.multiple_of(c * HEAD, HEAD), HEAD) if looped else column(c)
            for c in (h, heads + h)
        ]
        sources = [(stale[:, cols], stale[:, past], stale_bias)]
        if final:
            sources.append((fresh(1, cols), fresh(2, cols), fresh_bias))
        before = load_state(*state, h) if state else None
        _, total, summed = result = attend(fresh(0, cols), sources, before)
        if final:
            rounded = (summed / total).astype(jnp.bfloat16).astype(jnp.float32)
            gated = (rounded * gate[:, cols].astype(jnp.float32)).astype(jnp.bfloat16)
            for i, out in enumerate(outs):
                out[:, cols] = gated[i * tok : (i + 1) * tok]
        return result

    if looped:
        lax.fori_loop(0, heads, lambda h, _: one_head(h) and 0, 0)
        return
    parts = [one_head(h) for h in range(heads)]
    if not final:
        store_state(*rest, parts)


def collect_kernel(order, heads, *refs):
    wide = heads * HEAD
    slot, _ = place(len(order))
    for ref, d in zip(refs, order):
        start = jnp.bitwise_xor(slot, d) * wide
        refs[-1][:, pl.ds(pl.multiple_of(start, wide), wide)] = ref[...]


def body(
    q_fresh,
    k_fresh,
    v_fresh,
    q_gain,
    k_gain,
    stale_keys,
    stale_values,
    gate_table,
    assign,
    counts,
    timestep,
):
    bf16, f32, i32 = jnp.bfloat16, jnp.float32, jnp.int32
    device = lax.axis_index("seq")
    size = lax.axis_size("seq")
    tok, model_width = q_fresh.shape
    block_rows, wide = stale_keys.shape[1:]
    slots = model_width // wide
    blocks = size // slots
    heads = wide // HEAD
    order = [6, 4, 7, 5, 2, 3, 1, 0]
    sizes = [block_rows * n // 32 for n in (26, 28, 32)] if blocks == 2 else [block_rows]
    rare = sizes[2:]

    (which,) = call(
        functools.partial(choose_kernel, slots, blocks, sizes),
        "choose",
        [SMEM] * 2,
        [(SMEM, (1,), i32)],
        0,
        8 * (block_rows * wide + tok * model_width),
    )(assign, counts)

    halves = np.arange(HEAD, dtype=np.float64) % (HEAD // 2)
    steps = jnp.asarray((10000.0 ** (-2.0 * halves / HEAD)).astype(np.float32)[None])

    def exchange(arrays, order):
        return [to_partner(a, d, size) for a, d in zip(arrays, order)]

    def run(rows, operands):
        assign, counts, keys, values, q, k, v, q_gain, k_gain, gate_table, timestep = operands
        (packed,) = call(
            functools.partial(compact_kernel, slots, tok),
            "compact",
            [SMEM] * 2 + [VMEM] * 2,
            [(VMEM, (rows, 2 * wide), bf16)],
            4 * rows * block_rows * wide,
            4 * (rows + block_rows) * wide,
        )(assign, counts, keys, values)
        stale = [to_block(packed, s * slots, size) for s in range(1, blocks)]
        bundles = []
        for part in (order[: slots // 2], order[slots // 2 :]):
            bundles += call(
                functools.partial(norm_kernel, slots, part, heads),
                "norm",
                [SMEM] + [VMEM] * 6,
                [(VMEM, (3 * tok, wide), bf16)] * len(part),
                12 * tok * model_width,
                8 * tok * model_width,
            )(assign, q, k, v, q_gain[None], k_gain[None], steps)
        fresh = exchange(bundles, order)
        gate = lax.dynamic_slice(gate_table, (timestep[0], device % slots * wide), (1, wide))
        state = []

        def step(s, outs, extra):
            given = [*fresh, stale[s - 1], *state, *extra]
            return call(
                functools.partial(
                    attend_kernel, order, tok, blocks, heads, rows in rare, s, len(state)
                ),
                "attend",
                [SMEM] * 2 + [VMEM] * len(given),
                outs,
                8 * block_rows * block_rows * wide,
                16 * block_rows * wide,
            )(assign, counts, *given)

        for s in range(1, blocks - 1):
            state = step(s, [(VMEM, (block_rows, n), f32) for n in (HEAD, wide)], [])
        outs = step(blocks - 1, [(VMEM, (tok, wide), bf16)] * slots, [gate])
        back_order = [3, 1, 6, 7, 4, 5, 2, 0] if rows == sizes[0] else [6, 7, 4, 5, 2, 3, 1, 0]
        back = exchange([outs[order.index(d)] for d in back_order], back_order)
        new_keys, new_values = call(
            functools.partial(cache_kernel, order, tok),
            "cache",
            [VMEM] * slots,
            [(VMEM, (1, block_rows, wide), bf16)] * 2,
            0,
            8 * block_rows * wide,
        )(*fresh)
        (mixed,) = call(
            functools.partial(collect_kernel, back_order, heads),
            "collect",
            [VMEM] * len(back),
            [(VMEM, (tok, model_width), bf16)],
            0,
            4 * tok * model_width,
        )(*back)
        return mixed, new_keys, new_values

    operands = (
        assign,
        counts,
        stale_keys,
        stale_values,
        q_fresh,
        k_fresh,
        v_fresh,
        q_gain,
        k_gain,
        gate_table,
        timestep,
    )
    return lax.switch(which[0], [functools.partial(run, rows) for rows in sizes], operands)


def solution(mesh):
    rows = P(("groups", "seq"), None)
    entries = P(("groups", "seq"), None, None)
    return jax.shard_map(
        body,
        mesh=mesh,
        in_specs=(
            rows,
            rows,
            rows,
            P(),
            P(),
            entries,
            entries,
            P(),
            P("groups"),
            P("groups"),
            P("groups"),
        ),
        out_specs=(rows, entries, entries),
        check_vma=False,
    )
```

```python
import functools
import math

import jax
import jax.numpy as jnp
import numpy as np
from jax import lax
from jax.experimental import pallas as pl
from jax.experimental.pallas import tpu as pltpu
from jax.sharding import PartitionSpec as P

HEAD = 128
RMS_EPS = 1e-06
VMEM_BYTES = 32 * 1024 * 1024
SMEM, VMEM = pltpu.SMEM, pltpu.VMEM


def call(kernel, name, ins, outs, flops, n_bytes, scratch=()):
    shapes = [jax.ShapeDtypeStruct(shape, dtype) for _, shape, dtype in outs]
    return pl.pallas_call(
        kernel,
        out_shape=shapes,
        in_specs=[pl.BlockSpec(memory_space=m) for m in ins],
        out_specs=[pl.BlockSpec(memory_space=m) for m, _, _ in outs],
        scratch_shapes=scratch,
        compiler_params=pltpu.CompilerParams(vmem_limit_bytes=VMEM_BYTES),
        cost_estimate=pl.CostEstimate(flops=flops, bytes_accessed=n_bytes, transcendentals=0),
        name=name,
    )


def to_partner(value, distance, size):
    if distance == 0:
        return value
    return lax.ppermute(value, "seq", [(i, i ^ distance) for i in range(size)])


def to_block(value, distance, size):
    return lax.ppermute(value, "seq", [(i, (i + distance) % size) for i in range(size)])


def column(h):
    return slice(h * HEAD, (h + 1) * HEAD)


def place(slots):
    device = lax.axis_index("seq")
    return lax.rem(device, slots), lax.div(device, slots)


def live_of(assign, counts, index):
    return counts[assign[index]]


def live_lanes(assign, counts, tok, indices):
    width = tok * len(indices)
    lane = lax.broadcasted_iota(jnp.int32, (1, width), 1)
    count = jnp.zeros((1, width), jnp.int32)
    for i, index in enumerate(indices):
        count = jnp.where(lane // tok == i, live_of(assign, counts, index), count)
    return lane % tok, count


def choose_kernel(slots, blocks, sizes, assign, counts, out):
    most = jnp.int32(0)
    for b in range(blocks):
        total = jnp.int32(0)
        for i in range(slots):
            total = total + live_of(assign, counts, b * slots + i)
        most = jnp.maximum(most, total)
    which = jnp.int32(0)
    for n in sizes[:-1]:
        which = which + (most > n).astype(jnp.int32)
    out[0] = which


def compact_kernel(slots, tok, assign, counts, keys, values, out):
    rows, width, wide = out.shape[0], slots * tok, keys.shape[2]
    _, block = place(slots)
    indices = [block * slots + i for i in range(slots)]
    within, count = live_lanes(assign, counts, tok, indices)
    lane = lax.broadcasted_iota(jnp.int32, (1, width), 1)
    ahead = jnp.zeros((1, width), jnp.int32)
    for i, index in enumerate(indices):
        ahead = ahead + jnp.where(lane // tok > i, live_of(assign, counts, index), 0)
    goal = jnp.where(within < count, ahead + within, -1)
    row = lax.broadcasted_iota(jnp.int32, (rows, width), 0)
    pick = jnp.where(row == goal, 1.0, 0.0).astype(jnp.bfloat16)
    for part, ref in enumerate((keys, values)):
        moved = jnp.dot(pick, ref[0], preferred_element_type=jnp.float32)
        out[:, part * wide : (part + 1) * wide] = moved.astype(jnp.bfloat16)


def norm_kernel(slots, order, heads, assign, q, k, v, q_gain, k_gain, steps, *outs):
    tok, width = q.shape
    slot, block = place(slots)
    patch = assign[block * slots + slot]
    position = patch * tok + lax.broadcasted_iota(jnp.int32, (tok, HEAD), 0)
    angles = position.astype(jnp.float32) * steps[...]
    low = lax.broadcasted_iota(jnp.int32, (tok, HEAD), 1) < HEAD // 2
    cos_part = jnp.cos(angles)
    sin_part = jnp.sin(angles)
    sin_part = jnp.where(low, -sin_part, sin_part)

    def inverse(ref):
        total = jnp.zeros((tok, HEAD), jnp.float32)
        for c in range(0, width, HEAD):
            x = ref[:, c : c + HEAD].astype(jnp.float32)
            total = total + x * x
        return lax.rsqrt(jnp.sum(total, axis=1, keepdims=True) / width + RMS_EPS)

    scales = inverse(q), inverse(k)
    wide = heads * HEAD

    def one_head(h, _):
        to = pl.ds(pl.multiple_of(h * HEAD, HEAD), HEAD)
        for out, d in zip(outs, order):
            start = jnp.bitwise_xor(slot, d) * wide + h * HEAD
            col = pl.ds(pl.multiple_of(start, HEAD), HEAD)
            out[2 * tok : 3 * tok, to] = v[:, col]
            for part, (ref, gain) in enumerate(((q, q_gain), (k, k_gain))):
                x = ref[:, col].astype(jnp.float32) * scales[part]
                x = x * gain[:, col].astype(jnp.float32)
                turned = x * cos_part + pltpu.roll(x, HEAD // 2, 1) * sin_part
                out[part * tok : (part + 1) * tok, to] = turned.astype(jnp.bfloat16)
        return 0

    lax.fori_loop(0, heads, one_head, 0)


def cache_kernel(order, tok, *refs):
    new_keys, new_values = refs[len(order) :]
    slot, _ = place(len(order))
    for ref, d in zip(refs, order):
        at = pl.ds(pl.multiple_of(jnp.bitwise_xor(slot, d) * tok, tok), tok)
        new_keys[0, at, :] = ref[tok : 2 * tok, :]
        new_values[0, at, :] = ref[2 * tok : 3 * tok, :]


def attend(queries, sources, state):
    scale = HEAD**-0.5 / math.log(2.0)
    scores = [
        lax.dot_general(
            queries, keys, (((1,), (1,)), ((), ())), preferred_element_type=jnp.float32
        )
        + bias
        for keys, _, bias in sources
    ]
    tops = [jnp.max(s, axis=1, keepdims=True) for s in scores]
    top = functools.reduce(jnp.maximum, tops + ([] if state is None else [state[0]]))
    weights = [jnp.exp2(s * scale - top * scale) for s in scores]
    total = sum(jnp.sum(w, axis=1, keepdims=True) for w in weights)
    summed = sum(
        jnp.dot(w.astype(jnp.bfloat16), values, preferred_element_type=jnp.float32)
        for w, (_, values, _) in zip(weights, sources)
    )
    if state is not None:
        fading = jnp.exp2((state[0] - top) * scale)
        total = total + state[1] * fading
        summed = summed + state[2] * fading
    return top, total, summed


def store_state(stats, sums, parts):
    rows = parts[0][0].shape[0]
    lane = lax.broadcasted_iota(jnp.int32, (rows, HEAD), 1)
    packed = jnp.zeros((rows, HEAD), jnp.float32)
    for h, (top, total, summed) in enumerate(parts):
        packed = jnp.where(lane == h, top, packed)
        packed = jnp.where(lane == HEAD // 2 + h, total, packed)
        sums[:, column(h)] = summed
    stats[...] = packed


def load_state(stats, sums, h):
    half = HEAD // 2
    return stats[:, h : h + 1], stats[:, half + h : half + h + 1], sums[:, column(h)]


def attend_kernel(order, tok, blocks, heads, looped, step, n_state, assign, counts, *refs):
    slots = len(order)
    bundles, refs = refs[:slots], refs[slots:]
    stale, state, rest = refs[0], refs[1 : 1 + n_state], refs[1 + n_state :]
    final = step == blocks - 1
    slot, block = place(slots)
    source = lax.rem(block - step + blocks, blocks) * slots
    live = jnp.int32(0)
    for i in range(slots):
        live = live + live_of(assign, counts, source + i)
    lane = lax.broadcasted_iota(jnp.int32, (1, stale.shape[0]), 1)
    stale_bias = jnp.where(lane < live, 0.0, -jnp.inf)
    if final:
        gate, outs = rest[0], rest[1:]
        indices = [block * slots + jnp.bitwise_xor(slot, d) for d in order]
        within, count = live_lanes(assign, counts, tok, indices)
        fresh_bias = jnp.where(within < count, 0.0, -jnp.inf)

    def fresh(part, cols):
        return jnp.concatenate([r[part * tok : (part + 1) * tok, cols] for r in bundles], axis=0)

    def one_head(h):
        cols, past = [
            pl.ds(pl.multiple_of(c * HEAD, HEAD), HEAD) if looped else column(c)
            for c in (h, heads + h)
        ]
        sources = [(stale[:, cols], stale[:, past], stale_bias)]
        if final:
            sources.append((fresh(1, cols), fresh(2, cols), fresh_bias))
        before = load_state(*state, h) if state else None
        _, total, summed = result = attend(fresh(0, cols), sources, before)
        if final:
            rounded = (summed / total).astype(jnp.bfloat16).astype(jnp.float32)
            gated = (rounded * gate[:, cols].astype(jnp.float32)).astype(jnp.bfloat16)
            for i, out in enumerate(outs):
                out[:, cols] = gated[i * tok : (i + 1) * tok]
        return result

    if looped:
        lax.fori_loop(0, heads, lambda h, _: one_head(h) and 0, 0)
        return
    parts = [one_head(h) for h in range(heads)]
    if not final:
        store_state(*rest, parts)


def collect_kernel(order, heads, *refs):
    wide = heads * HEAD
    slot, _ = place(len(order))
    for ref, d in zip(refs, order):
        start = jnp.bitwise_xor(slot, d) * wide
        refs[-1][:, pl.ds(pl.multiple_of(start, wide), wide)] = ref[...]


def body(
    q_fresh,
    k_fresh,
    v_fresh,
    q_gain,
    k_gain,
    stale_keys,
    stale_values,
    gate_table,
    assign,
    counts,
    timestep,
):
    bf16, f32, i32 = jnp.bfloat16, jnp.float32, jnp.int32
    device = lax.axis_index("seq")
    size = lax.axis_size("seq")
    tok, model_width = q_fresh.shape
    block_rows, wide = stale_keys.shape[1:]
    slots = model_width // wide
    blocks = size // slots
    heads = wide // HEAD
    order = [6, 4, 7, 5, 2, 3, 1, 0]
    sizes = [block_rows * n // 32 for n in (27, 28, 32)] if blocks == 2 else [block_rows]
    rare = sizes[2:]

    (which,) = call(
        functools.partial(choose_kernel, slots, blocks, sizes),
        "choose",
        [SMEM] * 2,
        [(SMEM, (1,), i32)],
        0,
        8 * (block_rows * wide + tok * model_width),
    )(assign, counts)

    halves = np.arange(HEAD, dtype=np.float64) % (HEAD // 2)
    steps = jnp.asarray((10000.0 ** (-2.0 * halves / HEAD)).astype(np.float32)[None])

    def exchange(arrays, order):
        return [to_partner(a, d, size) for a, d in zip(arrays, order)]

    def run(rows, operands):
        assign, counts, keys, values, q, k, v, q_gain, k_gain, gate_table, timestep = operands
        (packed,) = call(
            functools.partial(compact_kernel, slots, tok),
            "compact",
            [SMEM] * 2 + [VMEM] * 2,
            [(VMEM, (rows, 2 * wide), bf16)],
            4 * rows * block_rows * wide,
            4 * (rows + block_rows) * wide,
        )(assign, counts, keys, values)
        stale = [to_block(packed, s * slots, size) for s in range(1, blocks)]
        bundles = []
        for part in (order[: slots // 2], order[slots // 2 :]):
            bundles += call(
                functools.partial(norm_kernel, slots, part, heads),
                "norm",
                [SMEM] + [VMEM] * 6,
                [(VMEM, (3 * tok, wide), bf16)] * len(part),
                12 * tok * model_width,
                8 * tok * model_width,
            )(assign, q, k, v, q_gain[None], k_gain[None], steps)
        fresh = exchange(bundles, order)
        gate = lax.dynamic_slice(gate_table, (timestep[0], device % slots * wide), (1, wide))
        state = []

        def step(s, outs, extra):
            given = [*fresh, stale[s - 1], *state, *extra]
            return call(
                functools.partial(
                    attend_kernel, order, tok, blocks, heads, rows in rare, s, len(state)
                ),
                "attend",
                [SMEM] * 2 + [VMEM] * len(given),
                outs,
                8 * block_rows * block_rows * wide,
                16 * block_rows * wide,
            )(assign, counts, *given)

        for s in range(1, blocks - 1):
            state = step(s, [(VMEM, (block_rows, n), f32) for n in (HEAD, wide)], [])
        outs = step(blocks - 1, [(VMEM, (tok, wide), bf16)] * slots, [gate])
        back_order = [3, 1, 6, 7, 4, 5, 2, 0] if rows == sizes[0] else [6, 7, 4, 5, 2, 3, 1, 0]
        back = exchange([outs[order.index(d)] for d in back_order], back_order)
        new_keys, new_values = call(
            functools.partial(cache_kernel, order, tok),
            "cache",
            [VMEM] * slots,
            [(VMEM, (1, block_rows, wide), bf16)] * 2,
            0,
            8 * block_rows * wide,
        )(*fresh)
        (mixed,) = call(
            functools.partial(collect_kernel, back_order, heads),
            "collect",
            [VMEM] * len(back),
            [(VMEM, (tok, model_width), bf16)],
            0,
            4 * tok * model_width,
        )(*back)
        return mixed, new_keys, new_values

    operands = (
        assign,
        counts,
        stale_keys,
        stale_values,
        q_fresh,
        k_fresh,
        v_fresh,
        q_gain,
        k_gain,
        gate_table,
        timestep,
    )
    return lax.switch(which[0], [functools.partial(run, rows) for rows in sizes], operands)


def solution(mesh):
    rows = P(("groups", "seq"), None)
    entries = P(("groups", "seq"), None, None)
    return jax.shard_map(
        body,
        mesh=mesh,
        in_specs=(
            rows,
            rows,
            rows,
            P(),
            P(),
            entries,
            entries,
            P(),
            P("groups"),
            P("groups"),
            P("groups"),
        ),
        out_specs=(rows, entries, entries),
        check_vma=False,
    )
```

```python
import functools
import math

import jax
import jax.numpy as jnp
import numpy as np
from jax import lax
from jax.experimental import pallas as pl
from jax.experimental.pallas import tpu as pltpu
from jax.sharding import PartitionSpec as P

HEAD = 128
RMS_EPS = 1e-06
VMEM_BYTES = 32 * 1024 * 1024
SMEM, VMEM = pltpu.SMEM, pltpu.VMEM


def call(kernel, name, ins, outs, flops, n_bytes, scratch=()):
    shapes = [jax.ShapeDtypeStruct(shape, dtype) for _, shape, dtype in outs]
    return pl.pallas_call(
        kernel,
        out_shape=shapes,
        in_specs=[pl.BlockSpec(memory_space=m) for m in ins],
        out_specs=[pl.BlockSpec(memory_space=m) for m, _, _ in outs],
        scratch_shapes=scratch,
        compiler_params=pltpu.CompilerParams(vmem_limit_bytes=VMEM_BYTES),
        cost_estimate=pl.CostEstimate(flops=flops, bytes_accessed=n_bytes, transcendentals=0),
        name=name,
    )


def to_partner(value, distance, size):
    if distance == 0:
        return value
    return lax.ppermute(value, "seq", [(i, i ^ distance) for i in range(size)])


def to_block(value, distance, size):
    return lax.ppermute(value, "seq", [(i, (i + distance) % size) for i in range(size)])


def column(h):
    return slice(h * HEAD, (h + 1) * HEAD)


def place(slots):
    device = lax.axis_index("seq")
    return lax.rem(device, slots), lax.div(device, slots)


def live_of(assign, counts, index):
    return counts[assign[index]]


def live_lanes(assign, counts, tok, indices):
    width = tok * len(indices)
    lane = lax.broadcasted_iota(jnp.int32, (1, width), 1)
    count = jnp.zeros((1, width), jnp.int32)
    for i, index in enumerate(indices):
        count = jnp.where(lane // tok == i, live_of(assign, counts, index), count)
    return lane % tok, count


def choose_kernel(slots, blocks, sizes, assign, counts, out):
    most = jnp.int32(0)
    for b in range(blocks):
        total = jnp.int32(0)
        for i in range(slots):
            total = total + live_of(assign, counts, b * slots + i)
        most = jnp.maximum(most, total)
    which = jnp.int32(0)
    for n in sizes[:-1]:
        which = which + (most > n).astype(jnp.int32)
    out[0] = which


def compact_kernel(slots, tok, assign, counts, keys, values, out):
    rows, width, wide = out.shape[0], slots * tok, keys.shape[2]
    _, block = place(slots)
    indices = [block * slots + i for i in range(slots)]
    within, count = live_lanes(assign, counts, tok, indices)
    lane = lax.broadcasted_iota(jnp.int32, (1, width), 1)
    ahead = jnp.zeros((1, width), jnp.int32)
    for i, index in enumerate(indices):
        ahead = ahead + jnp.where(lane // tok > i, live_of(assign, counts, index), 0)
    goal = jnp.where(within < count, ahead + within, -1)
    row = lax.broadcasted_iota(jnp.int32, (rows, width), 0)
    pick = jnp.where(row == goal, 1.0, 0.0).astype(jnp.bfloat16)
    for part, ref in enumerate((keys, values)):
        moved = jnp.dot(pick, ref[0], preferred_element_type=jnp.float32)
        out[:, part * wide : (part + 1) * wide] = moved.astype(jnp.bfloat16)


def norm_kernel(slots, order, heads, assign, q, k, v, q_gain, k_gain, steps, *outs):
    tok, width = q.shape
    slot, block = place(slots)
    patch = assign[block * slots + slot]
    position = patch * tok + lax.broadcasted_iota(jnp.int32, (tok, HEAD), 0)
    angles = position.astype(jnp.float32) * steps[...]
    low = lax.broadcasted_iota(jnp.int32, (tok, HEAD), 1) < HEAD // 2
    cos_part = jnp.cos(angles)
    sin_part = jnp.sin(angles)
    sin_part = jnp.where(low, -sin_part, sin_part)

    def inverse(ref):
        total = jnp.zeros((tok, HEAD), jnp.float32)
        for c in range(0, width, HEAD):
            x = ref[:, c : c + HEAD].astype(jnp.float32)
            total = total + x * x
        return lax.rsqrt(jnp.sum(total, axis=1, keepdims=True) / width + RMS_EPS)

    scales = inverse(q), inverse(k)
    wide = heads * HEAD

    def one_head(h, _):
        to = pl.ds(pl.multiple_of(h * HEAD, HEAD), HEAD)
        for out, d in zip(outs, order):
            start = jnp.bitwise_xor(slot, d) * wide + h * HEAD
            col = pl.ds(pl.multiple_of(start, HEAD), HEAD)
            out[2 * tok : 3 * tok, to] = v[:, col]
            for part, (ref, gain) in enumerate(((q, q_gain), (k, k_gain))):
                x = ref[:, col].astype(jnp.float32) * scales[part]
                x = x * gain[:, col].astype(jnp.float32)
                turned = x * cos_part + pltpu.roll(x, HEAD // 2, 1) * sin_part
                out[part * tok : (part + 1) * tok, to] = turned.astype(jnp.bfloat16)
        return 0

    lax.fori_loop(0, heads, one_head, 0)


def cache_kernel(order, tok, *refs):
    new_keys, new_values = refs[len(order) :]
    slot, _ = place(len(order))
    for ref, d in zip(refs, order):
        at = pl.ds(pl.multiple_of(jnp.bitwise_xor(slot, d) * tok, tok), tok)
        new_keys[0, at, :] = ref[tok : 2 * tok, :]
        new_values[0, at, :] = ref[2 * tok : 3 * tok, :]


def attend(queries, sources, state):
    scale = HEAD**-0.5 / math.log(2.0)
    scores = [
        lax.dot_general(
            queries, keys, (((1,), (1,)), ((), ())), preferred_element_type=jnp.float32
        )
        + bias
        for keys, _, bias in sources
    ]
    tops = [jnp.max(s, axis=1, keepdims=True) for s in scores]
    top = functools.reduce(jnp.maximum, tops + ([] if state is None else [state[0]]))
    weights = [jnp.exp2(s * scale - top * scale) for s in scores]
    total = sum(jnp.sum(w, axis=1, keepdims=True) for w in weights)
    summed = sum(
        jnp.dot(w.astype(jnp.bfloat16), values, preferred_element_type=jnp.float32)
        for w, (_, values, _) in zip(weights, sources)
    )
    if state is not None:
        fading = jnp.exp2((state[0] - top) * scale)
        total = total + state[1] * fading
        summed = summed + state[2] * fading
    return top, total, summed


def store_state(stats, sums, parts):
    rows = parts[0][0].shape[0]
    lane = lax.broadcasted_iota(jnp.int32, (rows, HEAD), 1)
    packed = jnp.zeros((rows, HEAD), jnp.float32)
    for h, (top, total, summed) in enumerate(parts):
        packed = jnp.where(lane == h, top, packed)
        packed = jnp.where(lane == HEAD // 2 + h, total, packed)
        sums[:, column(h)] = summed
    stats[...] = packed


def load_state(stats, sums, h):
    half = HEAD // 2
    return stats[:, h : h + 1], stats[:, half + h : half + h + 1], sums[:, column(h)]


def attend_kernel(order, tok, blocks, heads, looped, step, n_state, assign, counts, *refs):
    slots = len(order)
    bundles, refs = refs[:slots], refs[slots:]
    stale, state, rest = refs[0], refs[1 : 1 + n_state], refs[1 + n_state :]
    final = step == blocks - 1
    slot, block = place(slots)
    source = lax.rem(block - step + blocks, blocks) * slots
    live = jnp.int32(0)
    for i in range(slots):
        live = live + live_of(assign, counts, source + i)
    lane = lax.broadcasted_iota(jnp.int32, (1, stale.shape[0]), 1)
    stale_bias = jnp.where(lane < live, 0.0, -jnp.inf)
    if final:
        gate, outs = rest[0], rest[1:]
        indices = [block * slots + jnp.bitwise_xor(slot, d) for d in order]
        within, count = live_lanes(assign, counts, tok, indices)
        fresh_bias = jnp.where(within < count, 0.0, -jnp.inf)

    def fresh(part, cols):
        return jnp.concatenate([r[part * tok : (part + 1) * tok, cols] for r in bundles], axis=0)

    def one_head(h):
        cols, past = [
            pl.ds(pl.multiple_of(c * HEAD, HEAD), HEAD) if looped else column(c)
            for c in (h, heads + h)
        ]
        sources = [(stale[:, cols], stale[:, past], stale_bias)]
        if final:
            sources.append((fresh(1, cols), fresh(2, cols), fresh_bias))
        before = load_state(*state, h) if state else None
        _, total, summed = result = attend(fresh(0, cols), sources, before)
        if final:
            rounded = (summed / total).astype(jnp.bfloat16).astype(jnp.float32)
            gated = (rounded * gate[:, cols].astype(jnp.float32)).astype(jnp.bfloat16)
            for i, out in enumerate(outs):
                out[:, cols] = gated[i * tok : (i + 1) * tok]
        return result

    if looped:
        lax.fori_loop(0, heads, lambda h, _: one_head(h) and 0, 0)
        return
    parts = [one_head(h) for h in range(heads)]
    if not final:
        store_state(*rest, parts)


def collect_kernel(order, heads, *refs):
    wide = heads * HEAD
    slot, _ = place(len(order))
    for ref, d in zip(refs, order):
        start = jnp.bitwise_xor(slot, d) * wide
        refs[-1][:, pl.ds(pl.multiple_of(start, wide), wide)] = ref[...]


def body(
    q_fresh,
    k_fresh,
    v_fresh,
    q_gain,
    k_gain,
    stale_keys,
    stale_values,
    gate_table,
    assign,
    counts,
    timestep,
):
    bf16, f32, i32 = jnp.bfloat16, jnp.float32, jnp.int32
    device = lax.axis_index("seq")
    size = lax.axis_size("seq")
    tok, model_width = q_fresh.shape
    block_rows, wide = stale_keys.shape[1:]
    slots = model_width // wide
    blocks = size // slots
    heads = wide // HEAD
    order = [6, 4, 7, 5, 2, 3, 1, 0]
    sizes = [block_rows * n // 32 for n in (27, 28, 32)] if blocks == 2 else [block_rows]
    rare = sizes[3:]

    (which,) = call(
        functools.partial(choose_kernel, slots, blocks, sizes),
        "choose",
        [SMEM] * 2,
        [(SMEM, (1,), i32)],
        0,
        8 * (block_rows * wide + tok * model_width),
    )(assign, counts)

    halves = np.arange(HEAD, dtype=np.float64) % (HEAD // 2)
    steps = jnp.asarray((10000.0 ** (-2.0 * halves / HEAD)).astype(np.float32)[None])

    def exchange(arrays, order):
        return [to_partner(a, d, size) for a, d in zip(arrays, order)]

    def run(rows, operands):
        assign, counts, keys, values, q, k, v, q_gain, k_gain, gate_table, timestep = operands
        (packed,) = call(
            functools.partial(compact_kernel, slots, tok),
            "compact",
            [SMEM] * 2 + [VMEM] * 2,
            [(VMEM, (rows, 2 * wide), bf16)],
            4 * rows * block_rows * wide,
            4 * (rows + block_rows) * wide,
        )(assign, counts, keys, values)
        stale = [to_block(packed, s * slots, size) for s in range(1, blocks)]
        bundles = []
        for part in (order[: slots // 2], order[slots // 2 :]):
            bundles += call(
                functools.partial(norm_kernel, slots, part, heads),
                "norm",
                [SMEM] + [VMEM] * 6,
                [(VMEM, (3 * tok, wide), bf16)] * len(part),
                12 * tok * model_width,
                8 * tok * model_width,
            )(assign, q, k, v, q_gain[None], k_gain[None], steps)
        fresh = exchange(bundles, order)
        gate = lax.dynamic_slice(gate_table, (timestep[0], device % slots * wide), (1, wide))
        state = []

        def step(s, outs, extra):
            given = [*fresh, stale[s - 1], *state, *extra]
            return call(
                functools.partial(
                    attend_kernel, order, tok, blocks, heads, rows in rare, s, len(state)
                ),
                "attend",
                [SMEM] * 2 + [VMEM] * len(given),
                outs,
                8 * block_rows * block_rows * wide,
                16 * block_rows * wide,
            )(assign, counts, *given)

        for s in range(1, blocks - 1):
            state = step(s, [(VMEM, (block_rows, n), f32) for n in (HEAD, wide)], [])
        outs = step(blocks - 1, [(VMEM, (tok, wide), bf16)] * slots, [gate])
        back_order = [3, 1, 6, 7, 4, 5, 2, 0] if rows == sizes[0] else [6, 7, 4, 5, 2, 3, 1, 0]
        back = exchange([outs[order.index(d)] for d in back_order], back_order)
        new_keys, new_values = call(
            functools.partial(cache_kernel, order, tok),
            "cache",
            [VMEM] * slots,
            [(VMEM, (1, block_rows, wide), bf16)] * 2,
            0,
            8 * block_rows * wide,
        )(*fresh)
        (mixed,) = call(
            functools.partial(collect_kernel, back_order, heads),
            "collect",
            [VMEM] * len(back),
            [(VMEM, (tok, model_width), bf16)],
            0,
            4 * tok * model_width,
        )(*back)
        return mixed, new_keys, new_values

    operands = (
        assign,
        counts,
        stale_keys,
        stale_values,
        q_fresh,
        k_fresh,
        v_fresh,
        q_gain,
        k_gain,
        gate_table,
        timestep,
    )
    return lax.switch(which[0], [functools.partial(run, rows) for rows in sizes], operands)


def solution(mesh):
    rows = P(("groups", "seq"), None)
    entries = P(("groups", "seq"), None, None)
    return jax.shard_map(
        body,
        mesh=mesh,
        in_specs=(
            rows,
            rows,
            rows,
            P(),
            P(),
            entries,
            entries,
            P(),
            P("groups"),
            P("groups"),
            P("groups"),
        ),
        out_specs=(rows, entries, entries),
        check_vma=False,
    )
```
